32 devices in a mesh: group: 2 (over y), expert: 4 (over z), tensor: 2 (over x), node: 2 (over core).
Axes of the slice: x: 2, y: 2, z: 4, core: 2. Of those that a mesh axis runs over, the one named last changes fastest.
Arguments:
- tokens: bfloat16 [1024, 7168], P(('group', 'expert'), ('tensor', 'node')), parts along dimension 0, may hold values from -6 to 6
- expert_ids: int32 [1024, 2], P(('group', 'expert')), parts along dimension 0, may hold values from 0 to 3, all different within a row; in each aligned block of 128 rows (0 to 127, 128 to 255, ...) at most 128 rows name the same one
- gate_weights: float32 [1024, 2], P(('group', 'expert')), parts along dimension 0, may hold values from 0.1 to 1
- gate_weight: bfloat16 [4, 1792, 7168], P('expert', ('tensor', 'node')), may hold values from -0.0625 to 0.0625
- up_weight: bfloat16 [4, 1792, 7168], P('expert', ('tensor', 'node')), may hold values from -0.0625 to 0.0625
- down_weight: bfloat16 [4, 1792, 7168], P('expert', None, ('tensor', 'node')), may hold values from -0.125 to 0.125
Outputs:
- mixed: bfloat16 [1024, 7168], P(('group', 'expert'), ('tensor', 'node')), parts along dimension 0
The draws below stay inside these ranges and needn't reach their ends.
There are 2 independent parts, one for each index of `group`. The reference program is written for one: setup_inputs(seed, part) draws one part's arguments, and reference() takes and returns one part's arrays. A program takes and returns all parts, laid end to end along the dimension named above; an argument that names none is the same for every part. Nothing has to cross between parts.
Inputs may be any that keep to these rules, and one draw needn't show every extreme that they name: `expert_ids`: each token names 2 different experts; among the 128 tokens of one aligned block no expert is named by more than 128 tokens, and in every draw some expert is named by exactly 128 tokens of some block.
All inputs are finite; a program needn't handle non-finite values.
Results may differ from the reference program's by a relative error of at most 0.0058.
Values may be sent and summed in bfloat16 or wider, within the bound.
No kernel may reach another device: no remote copies, remote signals or barrier semaphores. Data moves between devices by JAX's collectives and lax.ppermute only.
A program may use at most 128 MiB of HBM per device.

```python
import math
import jax
import jax.numpy as jnp
import numpy as np
from jax import lax

D = 7168
FF = 1792
TOP_W = 2
TOK_DEV = 128
TOKENS = 512
EXPERTS = 4
CAP = 128
N_EXPERT = 4


def levels(key, shape, pieces, smallest, top_value):
    def one(dim, parts):
        draws = jax.random.uniform(jax.random.fold_in(jax.random.fold_in(key, 6), dim), (parts,), jnp.float32, smallest / len(pieces), top_value / len(pieces))
        return jnp.repeat(jnp.exp(draws), shape[dim] // parts).reshape((-1,) + (1,) * (len(shape) - dim - 1))

    factor_of = one(*pieces[0])
    for cut in pieces[1:]:
        factor_of = factor_of * one(*cut)
    return factor_of


def assign_block(rng, own, number, rows, count, top, bound, skew):
    order = jax.random.permutation(rng, count)
    crowded, usual = shares(count, rows * top, bound, skew, True), shares(count, rows * top, bound, skew, False)
    places = jnp.arange(count)

    def named(lengths, rotation):
        used = int((lengths > 0).sum())
        fixed = max(1, used // 4)
        moved = fixed + (places - fixed + rotation * (used - fixed)) % max(1, count - fixed)
        return jnp.zeros((count,), jnp.int32).at[order[jnp.where(places < fixed, places, moved)]].set(jnp.asarray(lengths, jnp.int32))

    lengths = jnp.where(number % 4 == 0, named(crowded, number // 4), named(usual, number - number // 4 - 1))
    mixed = jax.random.permutation(jax.random.fold_in(own, 3), count)
    giver, taker = mixed[0:count // 2 * 2:2], mixed[1:count // 2 * 2:2]
    margin = jnp.minimum(lengths[giver] - 1, bound - lengths[taker]) // 2
    margin = jnp.where((giver == order[0]) | (taker == order[0]) | (lengths[taker] == 0), 0, jnp.maximum(margin, 0))
    moved = jax.random.randint(jax.random.fold_in(own, 4), (count // 2,), 0, 1 << 20) % (margin + 1)
    lengths = lengths.at[giver].add(-moved).at[taker].add(moved)
    labels = jnp.searchsorted(jnp.cumsum(lengths), jnp.arange(rows * top), side="right").astype(jnp.int32)
    grid = labels.reshape(top, rows).T
    grid = grid[jax.random.permutation(jax.random.fold_in(own, 1), rows)]
    rotation = jax.random.randint(jax.random.fold_in(own, 2), (rows, 1), 0, top)
    return jnp.take_along_axis(grid, (jnp.arange(top)[None, :] + rotation) % top, axis=1)


def shares(number_of, total, reach, skew, full):
    loads = [(1 << 20) // math.isqrt(grade ** skew) + 1 for grade in range(1, number_of + 1)]
    largest = reach if full else min(reach, max(-(-total // number_of), total * loads[0] // sum(loads)))
    least = 1 if total - largest >= number_of - 1 else 0
    holding, surplus = [largest] + [least] * (number_of - 1), total - largest - least * (number_of - 1)
    while surplus > 0:
        free = [i for i in range(1, number_of) if holding[i] < largest] or [i for i in range(1, number_of) if holding[i] < reach]
        pool, remaining = sum([loads[i] for i in free]), surplus
        for i in free:
            addition = min(reach - holding[i], max(1, remaining * loads[i] // pool), surplus)
            holding[i] = holding[i] + addition
            surplus = surplus - addition
    return np.array(holding)


def scatter_about(own_key, extent, scale, limit, shards=(), kind=jnp.bfloat16):
    drawn = jax.random.normal(own_key, extent, jnp.float32) * scale
    if len(shards) > 0:
        drawn = levels(own_key, extent, shards, -0.22, 0.18) * drawn
    return jnp.clip(drawn, min=-limit, max=limit).astype(kind)


def setup_inputs(seed: int = 0, part: int = 0) -> dict:
    key_of = jax.random.split(jax.random.key(seed), 7)
    part_splits = jax.random.split(jax.random.fold_in(key_of[6], part), 7)
    tokens = scatter_about(part_splits[0], (TOKENS, D), 1.0, 6.0, ((0, 4), (1, 4)))
    expert_ids_keys = jax.random.split(jax.random.fold_in(part_splits[1], 1), TOKENS // TOK_DEV)
    expert_ids_turns = jax.random.permutation(jax.random.fold_in(part_splits[1], 3), TOKENS // TOK_DEV)
    expert_ids = jax.vmap(lambda own, number: assign_block(jax.random.fold_in(part_splits[1], 2), own, number, TOK_DEV, EXPERTS, TOP_W, CAP, 2))(expert_ids_keys, expert_ids_turns).reshape((TOKENS, TOP_W))
    gate_weights = jnp.clip(jnp.exp(math.log(1.0) - 2.3025851 * jax.random.uniform(part_splits[2], (TOKENS, TOP_W), jnp.float32) ** levels(part_splits[2], (TOKENS, TOP_W), ((0, 4),), -0.2, 0.2)), 0.1, 1.0)
    gate_weight = scatter_about(key_of[3], (EXPERTS, FF, D), D ** -0.5, 0.0625, ((0, 4), (1, 4)))
    up_weight = scatter_about(key_of[4], (EXPERTS, FF, D), D ** -0.5, 0.0625, ((0, 4), (1, 4)))
    down_weight = scatter_about(key_of[5], (EXPERTS, FF, D), FF ** -0.5, 0.125, ((0, 4), (2, 4)))
    return dict(tokens=tokens, expert_ids=expert_ids, gate_weights=gate_weights, gate_weight=gate_weight, up_weight=up_weight, down_weight=down_weight)


def positions_in_block(flat_ids):
    count = flat_ids.shape[0]
    one_hot = (flat_ids[:, None] == jnp.arange(EXPERTS, dtype=jnp.int32)[None, :]).astype(jnp.float32)
    earlier = (jnp.arange(count, dtype=jnp.int32)[:, None] > jnp.arange(count, dtype=jnp.int32)[None, :]).astype(jnp.float32)
    before = jnp.dot(earlier, one_hot, precision=lax.Precision.HIGHEST)
    return jnp.sum(before * one_hot, axis=1).astype(jnp.int32)


def reference(tokens, expert_ids, gate_weights, gate_weight, up_weight, down_weight):
    routes = TOK_DEV * TOP_W
    blocks = expert_ids.reshape(N_EXPERT, routes)
    position = jax.vmap(positions_in_block)(blocks)
    block_index = jnp.broadcast_to(jnp.arange(N_EXPERT, dtype=jnp.int32)[:, None], (N_EXPERT, routes))
    token_of = block_index * TOK_DEV + (jnp.arange(routes, dtype=jnp.int32) // TOP_W)[None, :]
    table = jnp.full((EXPERTS, N_EXPERT, CAP), TOKENS, jnp.int32)
    table = table.at[blocks, block_index, position].set(token_of.astype(jnp.int32))
    padded = jnp.concatenate([tokens, jnp.zeros((1, D), tokens.dtype)], axis=0)

    def one_expert(which):
        rows = jnp.take(padded, table[which].reshape(-1), axis=0)
        gate_part = jnp.dot(rows, gate_weight[which].T, preferred_element_type=jnp.float32)
        up_part = jnp.dot(rows, up_weight[which].T, preferred_element_type=jnp.float32)
        hidden = (jax.nn.silu(gate_part) * up_part).astype(jnp.bfloat16)
        result = jnp.dot(hidden, down_weight[which], preferred_element_type=jnp.float32).astype(jnp.bfloat16)
        return result.reshape(N_EXPERT, CAP, D)

    outputs = lax.map(one_expert, jnp.arange(EXPERTS, dtype=jnp.int32))
    picked = outputs[blocks, block_index, position].reshape(TOKENS, TOP_W, D)
    mixed = jnp.sum(picked.astype(jnp.float32) * gate_weights[:, :, None], axis=1)
    return mixed.astype(jnp.bfloat16)
```

```python
import functools

import jax
import jax.numpy as jnp
from jax import lax
from jax.experimental import pallas as pl
from jax.experimental.pallas import tpu as pltpu
from jax.sharding import PartitionSpec as P

MIB = 1 << 20


def route_positions(expert_ids, experts):
    flat_ids = expert_ids.reshape(-1)
    count = flat_ids.shape[0]
    one_hot = (flat_ids[:, None] == jnp.arange(experts, dtype=jnp.int32)[None, :]).astype(
        jnp.float32
    )
    earlier = (
        jnp.arange(count, dtype=jnp.int32)[:, None] > jnp.arange(count, dtype=jnp.int32)[None, :]
    ).astype(jnp.float32)
    before = jnp.dot(earlier, one_hot, precision=lax.Precision.HIGHEST)
    position = jnp.sum(before * one_hot, axis=1).astype(jnp.int32)
    return (flat_ids, position)


def slot_sources(target, top_slots, slots_total, count_rows):
    source_row = jnp.arange(target.shape[0], dtype=jnp.int32) // top_slots
    match = target[None, :] == jnp.arange(slots_total, dtype=jnp.int32)[:, None]
    picked = jnp.sum(jnp.where(match, source_row[None, :], 0), axis=1)
    filled = jnp.any(match, axis=1)
    return jnp.where(filled, picked, count_rows)


def pack_rows(rows, slot_table, experts, capacity):
    padded = jnp.concatenate([rows, jnp.zeros((1, rows.shape[1]), rows.dtype)], axis=0)
    return jnp.take(padded, slot_table, axis=0).reshape(experts, capacity, rows.shape[1])


def dispatch_shards(tokens, expert_ids, gate_weights, gate_weight, up_weight, down_weight):
    owners = lax.axis_size("expert")
    local_experts = gate_weight.shape[0]
    experts = local_experts * owners
    count_rows, top_slots = expert_ids.shape
    capacity = 2 * count_rows * top_slots // experts
    flat_ids, position = route_positions(expert_ids, experts)
    target = flat_ids * capacity + position
    slot_table = slot_sources(target, top_slots, experts * capacity, count_rows)
    whole = lax.all_gather(tokens, ("tensor", "node"), axis=1, tiled=True)
    packed = pack_rows(whole, slot_table, experts, capacity)
    received = lax.all_to_all(packed, "expert", split_axis=0, concat_axis=0, tiled=True)
    slots = received.shape[1]
    width = received.shape[2]
    grouped = received.reshape(owners, local_experts, slots, width)
    flat_rows = grouped[:, 0].reshape(owners * slots, width)
    contract = (((1,), (1,)), ((), ()))
    gate_part = lax.dot_general(
        flat_rows, gate_weight[0], contract, preferred_element_type=jnp.float32
    )
    up_part = lax.dot_general(flat_rows, up_weight[0], contract, preferred_element_type=jnp.float32)
    hidden = (jax.nn.silu(gate_part) * up_part).astype(jnp.bfloat16)
    block = down_weight[0]
    summed = jnp.dot(
        lax.all_gather(hidden, ("tensor", "node"), axis=1, tiled=True),
        block,
        preferred_element_type=jnp.float32,
    )
    results = [summed.astype(jnp.bfloat16).reshape(owners, slots, -1)]
    stacked = jnp.stack(results, axis=1).reshape(experts, slots, -1)
    returned = lax.all_to_all(stacked, "expert", split_axis=0, concat_axis=0, tiled=True)
    flat_out = returned.reshape(experts * capacity, -1)
    picked = jnp.take(flat_out, target, axis=0).reshape(count_rows, top_slots, -1)
    mixed = jnp.sum(picked.astype(jnp.float32) * gate_weights[:, :, None], axis=1)
    return mixed.astype(jnp.bfloat16)


def gate_up_kernel(splits, order_ref, *refs):
    pieces = refs[:4]
    gate_ref, up_ref, out_ref, gate_acc, up_acc = refs[4:]
    step = pl.program_id(0)
    width = gate_ref.shape[1]
    contract = (((1,), (1,)), ((), ()))

    @pl.when(step == 0)
    def _():
        gate_acc[...] = jnp.zeros_like(gate_acc)
        up_acc[...] = jnp.zeros_like(up_acc)

    for j in range(4 * splits):

        @pl.when(step == j)
        def _(j=j):
            part = j % splits
            rows = pieces[j // splits][:, part * width : (part + 1) * width]
            gate_acc[...] += lax.dot_general(
                rows, gate_ref[...], contract, preferred_element_type=jnp.float32
            )
            up_acc[...] += lax.dot_general(
                rows, up_ref[...], contract, preferred_element_type=jnp.float32
            )

    @pl.when(step == 4 * splits - 1)
    def _():
        gate = gate_acc[...]
        out_ref[...] = (gate / (1.0 + jnp.exp(-gate)) * up_acc[...]).astype(out_ref.dtype)


def gate_up(order, pieces, gate_weight, up_weight):
    rows, width = pieces[0].shape
    units = gate_weight.shape[0]
    splits = 2
    chunk = width // splits
    whole = pl.BlockSpec((rows, width), lambda k, order: (0, 0))
    weight = pl.BlockSpec(
        (units, chunk), lambda k, order: (0, order[k // splits] * splits + k % splits)
    )
    return pl.pallas_call(
        functools.partial(gate_up_kernel, splits),
        out_shape=jax.ShapeDtypeStruct((rows, units), jnp.bfloat16),
        grid_spec=pltpu.PrefetchScalarGridSpec(
            num_scalar_prefetch=1,
            grid=(4 * splits,),
            in_specs=[whole] * 4 + [weight] * 2,
            out_specs=pl.BlockSpec((rows, units), lambda k, order: (0, 0)),
            scratch_shapes=[pltpu.VMEM((rows, units), jnp.float32)] * 2,
        ),
        compiler_params=pltpu.CompilerParams(vmem_limit_bytes=24 * MIB),
        cost_estimate=pl.CostEstimate(
            flops=16 * rows * width * units,
            bytes_accessed=16 * width * units + 8 * rows * width,
            transcendentals=rows * units,
        ),
        name="gate_up",
    )(order, *pieces, gate_weight, up_weight)


def down_kernel(order_ref, *refs):
    pieces = refs[:4]
    weight_ref, out_ref, acc = refs[4:]
    step = pl.program_id(0)
    for j in range(4):

        @pl.when(step == j)
        def _(j=j):
            part = jnp.dot(pieces[j][...], weight_ref[...], preferred_element_type=jnp.float32)
            if j == 0:
                acc[...] = part
            elif j < 3:
                acc[...] += part
            else:
                out_ref[...] = (acc[...] + part).astype(out_ref.dtype)


def down(order, pieces, weight):
    rows, units = pieces[0].shape
    width = weight.shape[1]
    whole = pl.BlockSpec((rows, units), lambda k, order: (0, 0))
    return pl.pallas_call(
        down_kernel,
        out_shape=jax.ShapeDtypeStruct((rows, width), jnp.bfloat16),
        grid_spec=pltpu.PrefetchScalarGridSpec(
            num_scalar_prefetch=1,
            grid=(4,),
            in_specs=[whole] * 4 + [pl.BlockSpec((units, width), lambda k, order: (order[k], 0))],
            out_specs=pl.BlockSpec((rows, width), lambda k, order: (0, 0)),
            scratch_shapes=[pltpu.VMEM((rows, width), jnp.float32)],
        ),
        compiler_params=pltpu.CompilerParams(vmem_limit_bytes=16 * MIB),
        cost_estimate=pl.CostEstimate(
            flops=8 * rows * width * units,
            bytes_accessed=8 * width * units + 2 * rows * width,
            transcendentals=0,
        ),
        name="down",
    )(order, *pieces, weight)


SWAP = [(0, 1), (1, 0)]


def four_pieces(piece):
    across = lax.ppermute(piece, "tensor", SWAP)
    beside = lax.ppermute(piece, "node", SWAP)
    return (piece, across, beside, lax.ppermute(across, "node", SWAP))


def ring_shards(tokens, expert_ids, gate_weights, gate_weight, up_weight, down_weight):
    owners = lax.axis_size("expert")
    me = lax.axis_index("expert")
    tensor, node = lax.axis_index("tensor"), lax.axis_index("node")
    ring = [(i, (i + 1) % owners) for i in range(owners)]
    order = jnp.stack(
        [
            tensor * 2 + node,
            (1 - tensor) * 2 + node,
            tensor * 2 + 1 - node,
            (1 - tensor) * 2 + 1 - node,
        ]
    ).astype(jnp.int32)

    def weight_at(expert):
        return jnp.sum(jnp.where(expert_ids == expert, gate_weights, 0.0), axis=1)

    shares = [weight_at(me)]
    for s in range(1, owners):
        shift = [(i, (i + s) % owners) for i in range(owners)]
        column = weight_at(lax.rem(me + s, owners))
        shares.append(lax.ppermute(column.reshape(1, -1), "expert", shift).reshape(-1))

    blocks = [tokens]
    for s in range(1, owners):
        blocks.append(lax.ppermute(blocks[-1], "expert", ring))

    def contribution(s):
        hidden = gate_up(order, four_pieces(blocks[s]), gate_weight[0], up_weight[0])
        result = down(order, four_pieces(hidden), down_weight[0])
        share = shares[s][:, None]
        return jnp.where(share != 0, share * result.astype(jnp.float32), 0.0)

    own = contribution(0)
    partial = None
    for s in range(1, owners):
        term = contribution(s)
        if partial is not None:
            term = term + partial.astype(jnp.float32)
        partial = lax.ppermute(term.astype(jnp.bfloat16), "expert", ring)
    return (own + partial.astype(jnp.float32)).astype(jnp.bfloat16)


def shards(tokens, expert_ids, gate_weights, gate_weight, up_weight, down_weight):
    experts = gate_weight.shape[0] * lax.axis_size("expert")
    count_rows, top_slots = expert_ids.shape
    capacity = 2 * count_rows * top_slots // experts
    pairs = lax.axis_size("tensor") == 2 and lax.axis_size("node") == 2
    whole_blocks = capacity >= count_rows and gate_weight.shape[0] == 1
    body = ring_shards if pairs and whole_blocks else dispatch_shards
    return body(tokens, expert_ids, gate_weights, gate_weight, up_weight, down_weight)


def solution(mesh):
    placed = (
        P(("group", "expert"), ("tensor", "node")),
        P(("group", "expert"), None),
        P(("group", "expert"), None),
        P("expert", ("tensor", "node"), None),
        P("expert", ("tensor", "node"), None),
        P("expert", None, ("tensor", "node")),
    )
    return jax.shard_map(
        shards,
        mesh=mesh,
        in_specs=placed,
        out_specs=P(("group", "expert"), ("tensor", "node")),
        check_vma=False,
    )
```

```python
import functools

import jax
import jax.numpy as jnp
from jax import lax
from jax.experimental import pallas as pl
from jax.experimental.pallas import tpu as pltpu
from jax.sharding import PartitionSpec as P

MIB = 1 << 20


def route_positions(expert_ids, experts):
    flat_ids = expert_ids.reshape(-1)
    count = flat_ids.shape[0]
    one_hot = (flat_ids[:, None] == jnp.arange(experts, dtype=jnp.int32)[None, :]).astype(
        jnp.float32
    )
    earlier = (
        jnp.arange(count, dtype=jnp.int32)[:, None] > jnp.arange(count, dtype=jnp.int32)[None, :]
    ).astype(jnp.float32)
    before = jnp.dot(earlier, one_hot, precision=lax.Precision.HIGHEST)
    position = jnp.sum(before * one_hot, axis=1).astype(jnp.int32)
    return (flat_ids, position)


def slot_sources(target, top_slots, slots_total, count_rows):
    source_row = jnp.arange(target.shape[0], dtype=jnp.int32) // top_slots
    match = target[None, :] == jnp.arange(slots_total, dtype=jnp.int32)[:, None]
    picked = jnp.sum(jnp.where(match, source_row[None, :], 0), axis=1)
    filled = jnp.any(match, axis=1)
    return jnp.where(filled, picked, count_rows)


def pack_rows(rows, slot_table, experts, capacity):
    padded = jnp.concatenate([rows, jnp.zeros((1, rows.shape[1]), rows.dtype)], axis=0)
    return jnp.take(padded, slot_table, axis=0).reshape(experts, capacity, rows.shape[1])


def dispatch_shards(tokens, expert_ids, gate_weights, gate_weight, up_weight, down_weight):
    owners = lax.axis_size("expert")
    local_experts = gate_weight.shape[0]
    experts = local_experts * owners
    count_rows, top_slots = expert_ids.shape
    capacity = 2 * count_rows * top_slots // experts
    flat_ids, position = route_positions(expert_ids, experts)
    target = flat_ids * capacity + position
    slot_table = slot_sources(target, top_slots, experts * capacity, count_rows)
    whole = lax.all_gather(tokens, ("tensor", "node"), axis=1, tiled=True)
    packed = pack_rows(whole, slot_table, experts, capacity)
    received = lax.all_to_all(packed, "expert", split_axis=0, concat_axis=0, tiled=True)
    slots = received.shape[1]
    width = received.shape[2]
    grouped = received.reshape(owners, local_experts, slots, width)
    flat_rows = grouped[:, 0].reshape(owners * slots, width)
    contract = (((1,), (1,)), ((), ()))
    gate_part = lax.dot_general(
        flat_rows, gate_weight[0], contract, preferred_element_type=jnp.float32
    )
    up_part = lax.dot_general(flat_rows, up_weight[0], contract, preferred_element_type=jnp.float32)
    hidden = (jax.nn.silu(gate_part) * up_part).astype(jnp.bfloat16)
    block = down_weight[0]
    summed = jnp.dot(
        lax.all_gather(hidden, ("tensor", "node"), axis=1, tiled=True),
        block,
        preferred_element_type=jnp.float32,
    )
    results = [summed.astype(jnp.bfloat16).reshape(owners, slots, -1)]
    stacked = jnp.stack(results, axis=1).reshape(experts, slots, -1)
    returned = lax.all_to_all(stacked, "expert", split_axis=0, concat_axis=0, tiled=True)
    flat_out = returned.reshape(experts * capacity, -1)
    picked = jnp.take(flat_out, target, axis=0).reshape(count_rows, top_slots, -1)
    mixed = jnp.sum(picked.astype(jnp.float32) * gate_weights[:, :, None], axis=1)
    return mixed.astype(jnp.bfloat16)


ROWS = (((1,), (1,)), ((), ()))


def in_hbm(array):
    return pltpu.with_memory_space_constraint(array, pltpu.HBM)


def in_vmem(array):
    return pltpu.with_memory_space_constraint(array, pltpu.VMEM)


def load_kernel(count, *refs):
    sources, targets, sems = refs[:count], refs[-count - 1 : -1], refs[-1]
    refs[-count - 2][...] = jnp.zeros_like(refs[-count - 2])
    copies = [
        pltpu.make_async_copy(source, target, sems.at[i])
        for i, (source, target) in enumerate(zip(sources, targets))
    ]
    for copy in copies:
        copy.start()
    for copy in copies:
        copy.wait()


def load(arrays, *after):
    count = len(arrays)
    return pl.pallas_call(
        functools.partial(load_kernel, count),
        out_shape=[jax.ShapeDtypeStruct((8, 128), jnp.float32)]
        + [pltpu.VMEM(a.shape, a.dtype) for a in arrays],
        in_specs=[pl.BlockSpec(memory_space=pltpu.HBM)] * count
        + [pl.BlockSpec(memory_space=pl.ANY)] * len(after),
        out_specs=[pl.BlockSpec(memory_space=pltpu.VMEM)] * (count + 1),
        scratch_shapes=[pltpu.SemaphoreType.DMA((count,))],
        compiler_params=pltpu.CompilerParams(vmem_limit_bytes=1 * MIB),
        cost_estimate=pl.CostEstimate(
            flops=0, bytes_accessed=2 * sum(a.size * 2 for a in arrays), transcendentals=0
        ),
        name="load",
    )(*[in_hbm(a) for a in arrays], *after)


def gate_up_kernel(order_ref, *refs):
    pieces = refs[:4]
    gate_ref, up_ref = refs[4:6]
    out_ref = refs[-1]
    width = pieces[0].shape[1]
    gate = up = 0.0
    for j, piece in enumerate(pieces):
        columns = pl.ds(pl.multiple_of(order_ref[j] * width, width), width)
        rows = piece[...]
        gate += lax.dot_general(
            rows, gate_ref[:, columns], ROWS, preferred_element_type=jnp.float32
        )
        up += lax.dot_general(rows, up_ref[:, columns], ROWS, preferred_element_type=jnp.float32)
    out_ref[...] = (gate / (1.0 + jnp.exp(-gate)) * up).astype(out_ref.dtype)


def gate_up(order, pieces, gate_weight, up_weight, *after):
    rows, width = pieces[0].shape
    units = gate_weight.shape[0]
    whole = pl.BlockSpec(memory_space=pltpu.VMEM)
    apart = pl.BlockSpec(memory_space=pl.ANY)
    return pl.pallas_call(
        gate_up_kernel,
        out_shape=jax.ShapeDtypeStruct((rows, units), jnp.bfloat16),
        in_specs=[pl.BlockSpec(memory_space=pltpu.SMEM)] + [whole] * 6 + [apart] * len(after),
        out_specs=whole,
        compiler_params=pltpu.CompilerParams(vmem_limit_bytes=4 * MIB),
        cost_estimate=pl.CostEstimate(
            flops=16 * rows * width * units,
            bytes_accessed=16 * width * units + 8 * rows * width,
            transcendentals=rows * units,
        ),
        name="gate_up",
    )(order, *pieces, in_vmem(gate_weight), in_vmem(up_weight), *after)


def down_kernel(order_ref, *refs):
    pieces = refs[:4]
    weight_ref = refs[4]
    out_ref, blocks, sems = refs[-3:]
    units = pieces[0].shape[1]
    copies = []
    for j in range(4):
        rows = pl.ds(pl.multiple_of(order_ref[j] * units, units), units)
        copies.append(pltpu.make_async_copy(weight_ref.at[rows, :], blocks.at[j], sems.at[j]))
    for copy in copies:
        copy.start()
    total = 0.0
    for j, piece in enumerate(pieces):
        copies[j].wait()
        total += jnp.dot(piece[...], blocks[j], preferred_element_type=jnp.float32)
    out_ref[...] = total.astype(out_ref.dtype)


def down_kernel(order_ref, *refs):
    pieces = refs[:4]
    weight_ref, out_ref = refs[4:]
    units = pieces[0].shape[1]
    total = 0.0
    for j, piece in enumerate(pieces):
        block = weight_ref[pl.ds(pl.multiple_of(order_ref[j] * units, units), units), :]
        total += jnp.dot(piece[...], block, preferred_element_type=jnp.float32)
    out_ref[...] = total.astype(out_ref.dtype)


def down(order, pieces, weight):
    rows, units = pieces[0].shape
    width = weight.shape[1]
    whole = pl.BlockSpec(memory_space=pltpu.VMEM)
    return pl.pallas_call(
        down_kernel,
        out_shape=jax.ShapeDtypeStruct((rows, width), jnp.bfloat16),
        in_specs=[pl.BlockSpec(memory_space=pltpu.SMEM)] + [whole] * 5,
        out_specs=whole,
        compiler_params=pltpu.CompilerParams(vmem_limit_bytes=4 * MIB),
        cost_estimate=pl.CostEstimate(
            flops=8 * rows * width * units,
            bytes_accessed=8 * width * units + 2 * rows * width,
            transcendentals=0,
        ),
        name="down",
    )(order, *pieces, in_vmem(weight))


SWAP = [(0, 1), (1, 0)]


def after(array, *others):
    return lax.optimization_barrier((array, *others))[0]


def swap(array, axis, what):
    with jax.named_scope(what):
        return lax.ppermute(array, axis, SWAP)


def ring_shards(tokens, expert_ids, gate_weights, gate_weight, up_weight, down_weight):
    owners = lax.axis_size("expert")
    me = lax.axis_index("expert")
    tensor, node = lax.axis_index("tensor"), lax.axis_index("node")
    ring = [(i, (i + 1) % owners) for i in range(owners)]
    order = jnp.stack(
        [
            tensor * 2 + node,
            (1 - tensor) * 2 + node,
            tensor * 2 + 1 - node,
            (1 - tensor) * 2 + 1 - node,
        ]
    ).astype(jnp.int32)

    named = expert_ids[None, :, :] == jnp.arange(owners, dtype=jnp.int32)[:, None, None]
    dense = jnp.sum(jnp.where(named, gate_weights[None, :, :], 0.0), axis=2)
    mine = jnp.arange(owners, dtype=jnp.int32)[:, None] == me

    def onward(array, what, places=1):
        shift = [(i, (i + places) % owners) for i in range(owners)]
        with jax.named_scope(what):
            return lax.ppermute(array, "expert", shift)

    def quarters(own, beyond, what):
        return (
            own,
            beyond,
            swap(own, "node", what + "_c"),
            swap(beyond, "node", what + "_xc"),
        )

    blocks, across, hidden = [tokens], [swap(tokens, "tensor", "tokens0_x")], []
    blocks.append(onward(tokens, "tokens1_z"))
    shares = [dense] + [onward(dense, f"share{s}_z", s) for s in range(1, owners)]
    gate = up = out = None
    for s in range(1, owners):
        known = [across[s - 1], *shares[1:]] if s == 1 else [across[s - 1], hidden[s - 2]]
        across.append(swap(after(blocks[s], *known), "tensor", f"tokens{s}_x"))
        if s + 1 < owners:
            onto = after(blocks[s], *known)
            blocks.append(onward(onto, f"tokens{s + 1}_z"))
        k = s - 1
        own, beyond = after(blocks[k], *known, blocks[s]), after(across[k], *known, blocks[s])
        if s == 1:
            gate, up, out = after(gate_weight[0]), after(up_weight[0]), after(down_weight[0])
        hidden.append(gate_up(order, quarters(own, beyond, f"tokens{k}"), gate, up))
        across[s] = after(across[s], hidden[k])
    k = owners - 1
    hidden.append(gate_up(order, quarters(blocks[k], across[k], f"tokens{k}"), gate, up))

    def contribution(s):
        own = after(hidden[s], across[-1]) if s == 0 else hidden[s]
        beyond = swap(own, "tensor", f"hidden{s}_x")
        result = down(order, quarters(own, beyond, f"hidden{s}"), out)
        share = jnp.sum(jnp.where(mine, shares[s], 0.0), axis=0)[:, None]
        return jnp.where(share != 0, share * result.astype(jnp.float32), 0.0)

    partial = None
    for s in range(1, owners):
        term = contribution(s)
        if partial is not None:
            term = term + partial.astype(jnp.float32)
        partial = onward(term.astype(jnp.bfloat16), f"sum{s}_z")
    return (contribution(0) + partial.astype(jnp.float32)).astype(jnp.bfloat16)


def shards(tokens, expert_ids, gate_weights, gate_weight, up_weight, down_weight):
    experts = gate_weight.shape[0] * lax.axis_size("expert")
    count_rows, top_slots = expert_ids.shape
    capacity = 2 * count_rows * top_slots // experts
    pairs = lax.axis_size("tensor") == 2 and lax.axis_size("node") == 2
    whole_blocks = capacity >= count_rows and gate_weight.shape[0] == 1
    body = ring_shards if pairs and whole_blocks else dispatch_shards
    return body(tokens, expert_ids, gate_weights, gate_weight, up_weight, down_weight)


def solution(mesh):
    placed = (
        P(("group", "expert"), ("tensor", "node")),
        P(("group", "expert"), None),
        P(("group", "expert"), None),
        P("expert", ("tensor", "node"), None),
        P("expert", ("tensor", "node"), None),
        P("expert", None, ("tensor", "node")),
    )
    return jax.shard_map(
        shards,
        mesh=mesh,
        in_specs=placed,
        out_specs=P(("group", "expert"), ("tensor", "node")),
        check_vma=False,
    )
```

```python
import functools

import jax
import jax.numpy as jnp
from jax import lax
from jax.experimental import pallas as pl
from jax.experimental.pallas import tpu as pltpu
from jax.sharding import PartitionSpec as P

MIB = 1 << 20


def route_positions(expert_ids, experts):
    flat_ids = expert_ids.reshape(-1)
    count = flat_ids.shape[0]
    one_hot = (flat_ids[:, None] == jnp.arange(experts, dtype=jnp.int32)[None, :]).astype(
        jnp.float32
    )
    earlier = (
        jnp.arange(count, dtype=jnp.int32)[:, None] > jnp.arange(count, dtype=jnp.int32)[None, :]
    ).astype(jnp.float32)
    before = jnp.dot(earlier, one_hot, precision=lax.Precision.HIGHEST)
    position = jnp.sum(before * one_hot, axis=1).astype(jnp.int32)
    return (flat_ids, position)


def slot_sources(target, top_slots, slots_total, count_rows):
    source_row = jnp.arange(target.shape[0], dtype=jnp.int32) // top_slots
    match = target[None, :] == jnp.arange(slots_total, dtype=jnp.int32)[:, None]
    picked = jnp.sum(jnp.where(match, source_row[None, :], 0), axis=1)
    filled = jnp.any(match, axis=1)
    return jnp.where(filled, picked, count_rows)


def pack_rows(rows, slot_table, experts, capacity):
    padded = jnp.concatenate([rows, jnp.zeros((1, rows.shape[1]), rows.dtype)], axis=0)
    return jnp.take(padded, slot_table, axis=0).reshape(experts, capacity, rows.shape[1])


def dispatch_shards(tokens, expert_ids, gate_weights, gate_weight, up_weight, down_weight):
    owners = lax.axis_size("expert")
    local_experts = gate_weight.shape[0]
    experts = local_experts * owners
    count_rows, top_slots = expert_ids.shape
    capacity = 2 * count_rows * top_slots // experts
    flat_ids, position = route_positions(expert_ids, experts)
    target = flat_ids * capacity + position
    slot_table = slot_sources(target, top_slots, experts * capacity, count_rows)
    whole = lax.all_gather(tokens, ("tensor", "node"), axis=1, tiled=True)
    packed = pack_rows(whole, slot_table, experts, capacity)
    received = lax.all_to_all(packed, "expert", split_axis=0, concat_axis=0, tiled=True)
    slots = received.shape[1]
    width = received.shape[2]
    grouped = received.reshape(owners, local_experts, slots, width)
    flat_rows = grouped[:, 0].reshape(owners * slots, width)
    contract = (((1,), (1,)), ((), ()))
    gate_part = lax.dot_general(
        flat_rows, gate_weight[0], contract, preferred_element_type=jnp.float32
    )
    up_part = lax.dot_general(flat_rows, up_weight[0], contract, preferred_element_type=jnp.float32)
    hidden = (jax.nn.silu(gate_part) * up_part).astype(jnp.bfloat16)
    block = down_weight[0]
    summed = jnp.dot(
        lax.all_gather(hidden, ("tensor", "node"), axis=1, tiled=True),
        block,
        preferred_element_type=jnp.float32,
    )
    results = [summed.astype(jnp.bfloat16).reshape(owners, slots, -1)]
    stacked = jnp.stack(results, axis=1).reshape(experts, slots, -1)
    returned = lax.all_to_all(stacked, "expert", split_axis=0, concat_axis=0, tiled=True)
    flat_out = returned.reshape(experts * capacity, -1)
    picked = jnp.take(flat_out, target, axis=0).reshape(count_rows, top_slots, -1)
    mixed = jnp.sum(picked.astype(jnp.float32) * gate_weights[:, :, None], axis=1)
    return mixed.astype(jnp.bfloat16)


ROWS = (((1,), (1,)), ((), ()))


def in_vmem(array):
    return pltpu.with_memory_space_constraint(array, pltpu.VMEM)


def gate_up_kernel(order_ref, *refs):
    pieces = refs[:4]
    gate_ref, up_ref = refs[4:6]
    out_ref = refs[-1]
    width = pieces[0].shape[1]
    gate = up = 0.0
    for j, piece in enumerate(pieces):
        columns = pl.ds(pl.multiple_of(order_ref[j] * width, width), width)
        rows = piece[...]
        gate += lax.dot_general(
            rows, gate_ref[:, columns], ROWS, preferred_element_type=jnp.float32
        )
        up += lax.dot_general(rows, up_ref[:, columns], ROWS, preferred_element_type=jnp.float32)
    out_ref[...] = (gate / (1.0 + jnp.exp(-gate)) * up).astype(out_ref.dtype)


def gate_up(order, pieces, gate_weight, up_weight, *after):
    rows, width = pieces[0].shape
    units = gate_weight.shape[0]
    whole = pl.BlockSpec(memory_space=pltpu.VMEM)
    apart = pl.BlockSpec(memory_space=pl.ANY)
    return pl.pallas_call(
        gate_up_kernel,
        out_shape=jax.ShapeDtypeStruct((rows, units), jnp.bfloat16),
        in_specs=[pl.BlockSpec(memory_space=pltpu.SMEM)] + [whole] * 6 + [apart] * len(after),
        out_specs=whole,
        compiler_params=pltpu.CompilerParams(vmem_limit_bytes=4 * MIB),
        cost_estimate=pl.CostEstimate(
            flops=16 * rows * width * units,
            bytes_accessed=16 * width * units + 8 * rows * width,
            transcendentals=rows * units,
        ),
        name="gate_up",
    )(order, *pieces, in_vmem(gate_weight), in_vmem(up_weight), *after)


def down_kernel(order_ref, *refs):
    pieces = refs[:4]
    weight_ref, out_ref = refs[4:]
    units = pieces[0].shape[1]
    total = 0.0
    for j, piece in enumerate(pieces):
        block = weight_ref[pl.ds(pl.multiple_of(order_ref[j] * units, units), units), :]
        total += jnp.dot(piece[...], block, preferred_element_type=jnp.float32)
    out_ref[...] = total.astype(out_ref.dtype)


def down(order, pieces, weight):
    rows, units = pieces[0].shape
    width = weight.shape[1]
    whole = pl.BlockSpec(memory_space=pltpu.VMEM)
    return pl.pallas_call(
        down_kernel,
        out_shape=jax.ShapeDtypeStruct((rows, width), jnp.bfloat16),
        in_specs=[pl.BlockSpec(memory_space=pltpu.SMEM)] + [whole] * 5,
        out_specs=whole,
        compiler_params=pltpu.CompilerParams(vmem_limit_bytes=4 * MIB),
        cost_estimate=pl.CostEstimate(
            flops=8 * rows * width * units,
            bytes_accessed=8 * width * units + 2 * rows * width,
            transcendentals=0,
        ),
        name="down",
    )(order, *pieces, in_vmem(weight))


SWAP = [(0, 1), (1, 0)]


def after(array, *others):
    return lax.optimization_barrier((array, *others))[0]


def swap(array, axis, what):
    with jax.named_scope(what):
        return lax.ppermute(array, axis, SWAP)


def ring_shards(tokens, expert_ids, gate_weights, gate_weight, up_weight, down_weight):
    owners = lax.axis_size("expert")
    me = lax.axis_index("expert")
    tensor, node = lax.axis_index("tensor"), lax.axis_index("node")
    ring = [(i, (i + 1) % owners) for i in range(owners)]
    order = jnp.stack(
        [
            tensor * 2 + node,
            (1 - tensor) * 2 + node,
            tensor * 2 + 1 - node,
            (1 - tensor) * 2 + 1 - node,
        ]
    ).astype(jnp.int32)

    named = expert_ids[None, :, :] == jnp.arange(owners, dtype=jnp.int32)[:, None, None]
    dense = jnp.sum(jnp.where(named, gate_weights[None, :, :], 0.0), axis=2)
    mine = jnp.arange(owners, dtype=jnp.int32)[:, None] == me

    def onward(array, what, places=1):
        shift = [(i, (i + places) % owners) for i in range(owners)]
        with jax.named_scope(what):
            return lax.ppermute(array, "expert", shift)

    def quarters(own, beyond, what):
        return (
            own,
            beyond,
            swap(own, "node", what + "_c"),
            swap(beyond, "node", what + "_xc"),
        )

    gate, up, out = gate_weight[0], up_weight[0], down_weight[0]
    shares = [dense] + [onward(dense, f"share{s}_z", s) for s in range(1, owners)]
    blocks, across = [tokens], [swap(tokens, "tensor", "tokens0_x")]
    blocks.append(onward(tokens, "tokens1_z"))
    hidden, terms, partial = [None] * owners, [], None

    def into_hidden(s, own, beyond, *others):
        hidden[s] = gate_up(order, quarters(own, beyond, f"tokens{s}"), gate, up, *others)

    def contribution(s):
        own = hidden[s]
        beyond = swap(own, "tensor", f"hidden{s}_x")
        result = down(order, quarters(own, beyond, f"hidden{s}"), out)
        share = jnp.sum(jnp.where(mine, shares[s], 0.0), axis=0)[:, None]
        return jnp.where(share != 0, share * result.astype(jnp.float32), 0.0)

    known = [across[0], *shares[1:]]
    for s in range(1, owners):
        own = after(blocks[s], *known)
        across.append(swap(own, "tensor", f"tokens{s}_x"))
        if s + 1 < owners:
            blocks.append(onward(own, f"tokens{s + 1}_z"))
        if s > 1:
            across[s] = after(across[s], hidden[s - 1])
        into_hidden(s, own, across[s], *terms[-1:])
        term = contribution(s)
        if partial is not None:
            term = term + partial.astype(jnp.float32)
        terms.append(term.astype(jnp.bfloat16))
        partial = onward(terms[-1], f"sum{s}_z")
        known = [across[s]]
    into_hidden(0, tokens, across[0], *terms[-1:])
    return (contribution(0) + partial.astype(jnp.float32)).astype(jnp.bfloat16)


def shards(tokens, expert_ids, gate_weights, gate_weight, up_weight, down_weight):
    experts = gate_weight.shape[0] * lax.axis_size("expert")
    count_rows, top_slots = expert_ids.shape
    capacity = 2 * count_rows * top_slots // experts
    pairs = lax.axis_size("tensor") == 2 and lax.axis_size("node") == 2
    whole_blocks = capacity >= count_rows and gate_weight.shape[0] == 1
    body = ring_shards if pairs and whole_blocks else dispatch_shards
    return body(tokens, expert_ids, gate_weights, gate_weight, up_weight, down_weight)


def solution(mesh):
    placed = (
        P(("group", "expert"), ("tensor", "node")),
        P(("group", "expert"), None),
        P(("group", "expert"), None),
        P("expert", ("tensor", "node"), None),
        P("expert", ("tensor", "node"), None),
        P("expert", None, ("tensor", "node")),
    )
    return jax.shard_map(
        shards,
        mesh=mesh,
        in_specs=placed,
        out_specs=P(("group", "expert"), ("tensor", "node")),
        check_vma=False,
    )
```
